256 devices in a mesh: section: 4 (over x), row: 4 (over y), col: 16 (over z, core).
Axes of the slice: x: 4, y: 4, z: 8, core: 2. Of those that a mesh axis runs over, the one named last changes fastest.
Arguments:
- layer_input: bfloat16 [4, 512, 4096], P('section', 'col', 'row'), may hold values from -6 to 6
- output_grad: bfloat16 [4, 512, 4096], P('section', 'col', 'row'), may hold values from -6 to 6
- gate_weight: bfloat16 [4, 4096, 14336], P('section', 'row', 'col'), may hold values from -0.09375 to 0.09375
- up_weight: bfloat16 [4, 4096, 14336], P('section', 'row', 'col'), may hold values from -0.09375 to 0.09375
- down_weight: bfloat16 [4, 14336, 4096], P('section', 'col', 'row'), may hold values from -0.046875 to 0.046875
Outputs:
- grad_down: bfloat16 [4, 14336, 4096], P('section', 'col', 'row')
- grad_gate: bfloat16 [4, 4096, 14336], P('section', 'row', 'col')
- grad_up: bfloat16 [4, 4096, 14336], P('section', 'row', 'col')
- grad_received: bfloat16 [4, 512, 4096], P('section', 'col', 'row')
The draws below stay inside these ranges and needn't reach their ends.
All inputs are finite; a program needn't handle non-finite values.
Results may differ from the reference program's by a relative error of at most 0.005.
Values may be sent and summed in bfloat16 or wider, within the bound.
A program may use at most 64 MiB of HBM per device.

```python
import jax
import jax.numpy as jnp

D = 4096
FF = 14336
TOK = 512
SECTIONS = 4


def levels(rng, shape, shards, smallest, high):
    loudness = 1.0
    for position, blocks in shards:
        draws = jax.random.uniform(jax.random.fold_in(jax.random.fold_in(rng, 6), position), (blocks,), jnp.float32, smallest / len(shards), high / len(shards))
        loudness = loudness * jnp.repeat(jnp.exp(draws), shape[position] // blocks).reshape((-1,) + (1,) * (len(shape) - 1 - position))
    return loudness


def centred(own_key, extent, deviation, limit, shards=(), held_as=jnp.bfloat16):
    entries = deviation * jax.random.normal(own_key, extent, jnp.float32)
    if shards:
        entries = entries * levels(own_key, extent, shards, -0.22, 0.18)
    return jnp.clip(entries, -limit, limit).astype(held_as)


def setup_inputs(seed: int = 0) -> dict:
    arg_keys = jax.random.split(jax.random.key(seed), 6)
    layer_input = centred(arg_keys[0], (SECTIONS, TOK, D), 1.0, 6.0, ((0, 4), (1, 16), (2, 4)))
    output_grad = centred(arg_keys[1], (SECTIONS, TOK, D), 1.0, 6.0, ((0, 4), (1, 16), (2, 4)))
    gate_weight = centred(arg_keys[2], (SECTIONS, D, FF), D ** -0.5, 0.09375, ((0, 4), (1, 4), (2, 16)))
    up_weight = centred(arg_keys[3], (SECTIONS, D, FF), D ** -0.5, 0.09375, ((0, 4), (1, 4), (2, 16)))
    down_weight = centred(arg_keys[4], (SECTIONS, FF, D), FF ** -0.5, 0.046875, ((0, 4), (1, 16), (2, 4)))
    return {"layer_input": layer_input, "output_grad": output_grad, "gate_weight": gate_weight, "up_weight": up_weight, "down_weight": down_weight}


def segment_backward(inputs, grads, w_gate, w_up, w_down):
    gate = jnp.dot(inputs, w_gate, preferred_element_type=jnp.float32)
    up = jnp.dot(inputs, w_up, preferred_element_type=jnp.float32)
    grad_hidden = jnp.dot(grads, w_down.T, preferred_element_type=jnp.float32)
    sig = jax.nn.sigmoid(gate)
    hidden = (gate * sig * up).astype(jnp.bfloat16)
    grad_gate_in = (grad_hidden * up * sig * (1.0 + gate * (1.0 - sig))).astype(jnp.bfloat16)
    grad_up_in = (grad_hidden * gate * sig).astype(jnp.bfloat16)
    grad_down = jnp.dot(hidden.T, grads, preferred_element_type=jnp.float32).astype(jnp.bfloat16)
    grad_gate = jnp.dot(inputs.T, grad_gate_in, preferred_element_type=jnp.float32).astype(jnp.bfloat16)
    grad_up = jnp.dot(inputs.T, grad_up_in, preferred_element_type=jnp.float32).astype(jnp.bfloat16)
    input_grad = jnp.dot(grad_gate_in, w_gate.T, preferred_element_type=jnp.float32)
    input_grad = input_grad + jnp.dot(grad_up_in, w_up.T, preferred_element_type=jnp.float32)
    return grad_down, grad_gate, grad_up, input_grad.astype(jnp.bfloat16)


def reference(layer_input, output_grad, gate_weight, up_weight, down_weight):
    results = [segment_backward(layer_input[s], output_grad[s], gate_weight[s], up_weight[s], down_weight[s]) for s in range(SECTIONS)]
    grad_down = jnp.stack([item[0] for item in results])
    grad_gate = jnp.stack([item[1] for item in results])
    grad_up = jnp.stack([item[2] for item in results])
    input_grad = jnp.stack([item[3] for item in results])
    grad_received = jnp.roll(input_grad, -1, axis=0)
    return grad_down, grad_gate, grad_up, grad_received
```

```python
import functools

import jax
import jax.numpy as jnp
from jax import lax
from jax.experimental import pallas as pl
from jax.experimental.pallas import tpu as pltpu
from jax.sharding import PartitionSpec as P

MESH = pl.DeviceIdType.MESH
F32 = jnp.float32
BF16 = jnp.bfloat16

LAG_MID, LAG_SUM, LAG_FWD, LAG_GRAD, LAG_ACC, LAG_OUT = 1, 3, 4, 6, 7, 7


def contract_cols(left, right):
    return lax.dot_general(left, right, (((1,), (1,)), ((), ())), preferred_element_type=F32)


def contract_rows(left, right):
    return lax.dot_general(left, right, (((0,), (0,)), ((), ())), preferred_element_type=F32)


def kernel(
    sizes,
    x_hbm, g_hbm, wg_hbm, wu_hbm, wd_hbm,
    od_hbm, og_hbm, ou_hbm, or_ref,
    wg, wu, wd, xg, part, opp_out, near_out, opp_in, near_in, mid_out, mid_in, h,
    acc_g, acc_u, acc_d, dg_out, dg_in, fin_out, fin_in, st_g, st_u, st_d,
    load_sem, store_sem,
    z_s, z_r, sib_s, sib_r, opp_s, opp_r, near_s, near_r, mid_s, mid_r, ag_s, ag_r, dg_s, dg_r, fin_s, fin_r,
):
    n_sec, n_row, n_col = sizes
    n_z = n_col // 2
    chunks = n_z
    tok = x_hbm.shape[1]
    span = 2 * tok
    quarter = span // n_row
    feat, width = wg.shape
    sec, row, col = lax.axis_index("section"), lax.axis_index("row"), lax.axis_index("col")
    core, z = col % 2, col // 2
    sibling = {"col": col + 1 - 2 * core}
    before = (sec + n_sec - 1) % n_sec
    after = (sec + 1) % n_sec

    def rows(start, size):
        return pl.ds(pl.multiple_of(start, size), size)

    def turn(k):
        return 1 - 2 * (k % 2)

    def at_row(shift):
        return (row + shift + n_row) % n_row

    def offset(k):
        return -((k + 1) // 2) * turn(k)

    def remote(src, dst, send, recv, device):
        return pltpu.make_async_remote_copy(
            src_ref=src, dst_ref=dst, send_sem=send, recv_sem=recv, device_id=device, device_id_type=MESH
        )

    own = rows(tok * core, tok)
    loads = [
        pltpu.make_async_copy(x_hbm.at[0], xg.at[0, own], load_sem.at[0]),
        pltpu.make_async_copy(g_hbm.at[0], xg.at[1, own], load_sem.at[1]),
        pltpu.make_async_copy(wg_hbm.at[0], wg, load_sem.at[2]),
        pltpu.make_async_copy(wu_hbm.at[0], wu, load_sem.at[3]),
        pltpu.make_async_copy(wd_hbm.at[0], wd, load_sem.at[4]),
    ]
    for load in loads:
        load.start()

    barrier = pltpu.get_barrier_semaphore()

    def greet(device):
        pl.semaphore_signal(barrier, inc=1, device_id=device, device_id_type=MESH)

    greet(sibling)
    greet({"row": at_row(1)})
    greet({"row": at_row(-1)})

    def greet_z(j, _):
        other = 2 * ((z + j) % n_z) + core

        @pl.when(j > 0)
        def _():
            greet({"col": other})

        greet({"section": before, "col": other})
        greet({"section": after, "col": other})
        return 0

    lax.fori_loop(0, n_z, greet_z, 0)

    acc_g[...] = jnp.zeros_like(acc_g)
    acc_u[...] = jnp.zeros_like(acc_u)
    acc_d[...] = jnp.zeros_like(acc_d)
    loads[0].wait()
    loads[1].wait()
    pl.semaphore_wait(barrier, 3 * n_z + 2)

    def to_sibling(k, half):
        place = rows(span * k + tok * half, tok)
        return remote(xg.at[:, place], xg.at[:, place], sib_s.at[k], sib_r.at[k], sibling)

    def along_z(k):
        place = rows(span * k + tok * core, tok)
        target = (z - offset(k) + n_z) % n_z
        return remote(xg.at[:, own], xg.at[:, place], z_s.at[k], z_r.at[k], {"col": 2 * target + core})

    def opp_copy(k):
        place = rows(quarter * k, quarter)
        return remote(opp_out.at[place], opp_in.at[place], opp_s.at[k], opp_r.at[k], {"row": at_row(turn(k))})

    def near_copy(k):
        place = rows(quarter * k, quarter)
        return remote(near_out.at[place], near_in.at[place], near_s.at[k], near_r.at[k], {"row": at_row(-turn(k))})

    def mid_copy(k):
        place = rows(quarter * k, quarter)
        return remote(mid_out.at[place], mid_in.at[place], mid_s.at[k], mid_r.at[k], {"row": at_row(turn(k))})

    def piece(k, owner):
        return rows(span * k + quarter * owner, quarter)

    def ag_copy(k, slot, owner, target):
        place = piece(k, owner)
        return remote(h.at[place], h.at[place], ag_s.at[3 * k + slot], ag_r.at[3 * k + slot], {"row": target})

    def dg_copy(k):
        return remote(dg_out.at[k], dg_in.at[k], dg_s.at[k], dg_r.at[k], sibling)

    def fin_copy(k):
        target = (z + offset(k) + n_z) % n_z
        return remote(
            fin_out.at[k], fin_in.at[k], fin_s.at[k], fin_r.at[k], {"section": before, "col": 2 * target + core}
        )

    def forward(k):
        to_sibling(k, 1 - core).wait_recv()
        place = rows(span * k, span)
        x, g = xg[0, place, :], xg[1, place, :]

        @pl.when(k == 0)
        def _():
            loads[2].wait()

        part[place, :width] = jnp.dot(x, wg[...], preferred_element_type=F32)

        @pl.when(k == 0)
        def _():
            loads[3].wait()

        part[place, width : 2 * width] = jnp.dot(x, wu[...], preferred_element_type=F32)

        @pl.when(k == 0)
        def _():
            loads[4].wait()

        part[place, 2 * width :] = contract_cols(g, wd[...])
        slot = rows(quarter * k, quarter)
        opp_out[slot] = part[piece(k, at_row(2)), :].astype(BF16)
        opp_copy(k).start()
        near_out[slot] = part[piece(k, at_row(-turn(k))), :].astype(BF16)
        near_copy(k).start()

    def middle(k):
        slot = rows(quarter * k, quarter)
        opp_copy(k).wait_recv()
        mid_out[slot] = (part[piece(k, at_row(turn(k))), :] + opp_in[slot].astype(F32)).astype(BF16)
        mid_copy(k).start()

    def sums(k):
        slot = rows(quarter * k, quarter)
        near_copy(k).wait_recv()
        mid_copy(k).wait_recv()
        mine = piece(k, row)
        total = part[mine, :] + near_in[slot].astype(F32) + mid_in[slot].astype(F32)
        gate, up, grad_hidden = total[:, :width], total[:, width : 2 * width], total[:, 2 * width :]
        sig = jax.nn.sigmoid(gate)
        h[mine, :width] = (grad_hidden * up * sig * (1.0 + gate * (1.0 - sig))).astype(BF16)
        h[mine, width : 2 * width] = (grad_hidden * gate * sig).astype(BF16)
        h[mine, 2 * width :] = (gate * sig * up).astype(BF16)
        ag_copy(k, 0, row, at_row(-turn(k))).start()
        ag_copy(k, 1, row, at_row(turn(k))).start()

    def onward(k):
        ag_copy(k, 0, at_row(turn(k)), row).wait_recv()
        ag_copy(k, 2, at_row(turn(k)), at_row(-turn(k))).start()

    def input_grad(k):
        ag_copy(k, 1, at_row(-turn(k)), row).wait_recv()
        ag_copy(k, 2, at_row(2), row).wait_recv()
        place = rows(span * k, span)
        part[place, :feat] = contract_cols(h[place, :width], wg[...]) + contract_cols(
            h[place, width : 2 * width], wu[...]
        )
        dg_out[k] = part[rows(span * k + tok * (1 - core), tok), :feat]
        dg_copy(k).start()

    def send_grad(k):
        dg_copy(k).wait_recv()
        fin_out[k] = (part[rows(span * k + tok * core, tok), :feat] + dg_in[k]).astype(BF16)
        fin_copy(k).start()

    def pair(k):
        return rows(span * (k - 1), 2 * span)

    def accumulate(k):
        place = pair(k)
        acc_g[...] += contract_rows(xg[0, place, :], h[place, :width])
        acc_u[...] += contract_rows(xg[0, place, :], h[place, width : 2 * width])
        acc_d[...] += contract_rows(h[place, 2 * width :], xg[1, place, :])

    def stage(i, lag, run, extra=None):
        k = i - lag
        ok = (k >= 0) & (k < chunks)
        if extra is not None:
            ok = ok & extra(k)

        @pl.when(ok)
        def _():
            run(k)

    to_sibling(0, core).start()
    along_z(1).start()
    along_z(2).start()

    def step(i, _):
        stage(i, 0, forward)

        @pl.when(i + 3 < chunks)
        def _():
            along_z(i + 3).start()

        stage(i, LAG_SUM, sums)
        stage(i, LAG_ACC, accumulate, lambda k: (k % 2 == 1) & (k < chunks - 1))
        stage(i, LAG_MID, middle)
        stage(i, LAG_OUT, send_grad)
        stage(i, LAG_GRAD, input_grad)
        stage(i, LAG_FWD, onward)

        @pl.when(i + 1 < chunks)
        def _():
            along_z(i + 1).wait_recv()
            to_sibling(i + 1, core).start()

        return 0

    lax.fori_loop(0, chunks + LAG_GRAD, step, 0)

    last = chunks - 1
    place = pair(last)
    st_g[...] = (acc_g[...] + contract_rows(xg[0, place, :], h[place, :width])).astype(BF16)
    stores = [
        pltpu.make_async_copy(st_g, og_hbm.at[0], store_sem.at[0]),
        pltpu.make_async_copy(st_u, ou_hbm.at[0], store_sem.at[1]),
        pltpu.make_async_copy(st_d, od_hbm.at[0], store_sem.at[2]),
    ]
    stores[0].start()
    send_grad(last)
    st_u[...] = (acc_u[...] + contract_rows(xg[0, place, :], h[place, width : 2 * width])).astype(BF16)
    stores[1].start()
    st_d[...] = (acc_d[...] + contract_rows(h[place, 2 * width :], xg[1, place, :])).astype(BF16)
    stores[2].start()

    def sent(k, _):
        @pl.when(k > 0)
        def _():
            along_z(k).wait_send()

        to_sibling(k, core).wait_send()
        opp_copy(k).wait_send()
        near_copy(k).wait_send()
        mid_copy(k).wait_send()
        ag_copy(k, 0, row, at_row(-turn(k))).wait_send()
        ag_copy(k, 1, row, at_row(turn(k))).wait_send()
        ag_copy(k, 2, at_row(turn(k)), at_row(-turn(k))).wait_send()
        dg_copy(k).wait_send()
        fin_copy(k).wait_send()
        fin_copy(k).wait_recv()
        return 0

    lax.fori_loop(0, chunks, sent, 0)
    total = fin_in[0].astype(F32)
    for k in range(1, chunks):
        total = total + fin_in[k].astype(F32)
    or_ref[0] = total.astype(BF16)
    for store in stores:
        store.wait()


def shards(sizes, layer_input, output_grad, gate_weight, up_weight, down_weight):
    tok, feat = layer_input.shape[1:]
    width = gate_weight.shape[2]
    chunks = sizes[2] // 2
    span = 2 * tok
    total = span * chunks
    quarter_rows = total // sizes[1]
    dma = pltpu.SemaphoreType.DMA
    shapes = [
        jax.ShapeDtypeStruct((1, width, feat), BF16),
        jax.ShapeDtypeStruct((1, feat, width), BF16),
        jax.ShapeDtypeStruct((1, feat, width), BF16),
        jax.ShapeDtypeStruct((1, tok, feat), BF16),
    ]
    return pl.pallas_call(
        functools.partial(kernel, sizes),
        out_shape=shapes,
        in_specs=[pl.BlockSpec(memory_space=pl.ANY)] * 5,
        out_specs=[pl.BlockSpec(memory_space=pl.ANY)] * 3 + [pl.BlockSpec(memory_space=pltpu.VMEM)],
        scratch_shapes=[
            pltpu.VMEM((feat, width), BF16),
            pltpu.VMEM((feat, width), BF16),
            pltpu.VMEM((width, feat), BF16),
            pltpu.VMEM((2, total, feat), BF16),
            pltpu.VMEM((total, 3 * width), F32),
        ]
        + [pltpu.VMEM((quarter_rows, 3 * width), BF16)] * 6
        + [
            pltpu.VMEM((total, 3 * width), BF16),
            pltpu.VMEM((feat, width), F32),
            pltpu.VMEM((feat, width), F32),
            pltpu.VMEM((width, feat), F32),
            pltpu.VMEM((chunks, tok, feat), F32),
            pltpu.VMEM((chunks, tok, feat), F32),
            pltpu.VMEM((chunks, tok, feat), BF16),
            pltpu.VMEM((chunks, tok, feat), BF16),
            pltpu.VMEM((feat, width), BF16),
            pltpu.VMEM((feat, width), BF16),
            pltpu.VMEM((width, feat), BF16),
            dma((5,)),
            dma((3,)),
        ]
        + [dma((chunks,))] * 10
        + [dma((3 * chunks,))] * 2
        + [dma((chunks,))] * 4,
        compiler_params=pltpu.CompilerParams(
            collective_id=0, has_side_effects=True, vmem_limit_bytes=58 * 1024 * 1024
        ),
    )(layer_input, output_grad, gate_weight, up_weight, down_weight)


def solution(mesh):
    sizes = tuple(mesh.shape[axis] for axis in ("section", "row", "col"))
    return jax.shard_map(
        functools.partial(shards, sizes),
        mesh=mesh,
        in_specs=(
            P("section", "col", "row"),
            P("section", "col", "row"),
            P("section", "row", "col"),
            P("section", "row", "col"),
            P("section", "col", "row"),
        ),
        out_specs=(
            P("section", "col", "row"),
            P("section", "row", "col"),
            P("section", "row", "col"),
            P("section", "col", "row"),
        ),
        check_vma=False,
    )
```

```python
import functools

import jax
import jax.numpy as jnp
from jax import lax
from jax.experimental import pallas as pl
from jax.experimental.pallas import tpu as pltpu
from jax.sharding import PartitionSpec as P

MESH = pl.DeviceIdType.MESH
F32 = jnp.float32
BF16 = jnp.bfloat16

LAG_MID, LAG_SUM, LAG_FWD, LAG_GRAD, LAG_ACC, LAG_OUT = 2, 4, 6, 9, 9, 10
LAG_HID, LAG_HID_FWD, LAG_DOWN = 9, 13, 21


def contract_cols(left, right):
    return lax.dot_general(left, right, (((1,), (1,)), ((), ())), preferred_element_type=F32)


def contract_rows(left, right):
    return lax.dot_general(left, right, (((0,), (0,)), ((), ())), preferred_element_type=F32)


def kernel(
    sizes,
    x_hbm, g_hbm, wg_hbm, wu_hbm, wd_hbm,
    st_d, st_g, st_u, or_ref,
    wg, wu, wd, xg, part, opp_out, near_out, opp_in, near_in, mid_out, mid_in, h, hid,
    acc_g, acc_u, acc_d, dg_out, dg_in, fin_out, fin_in,
    load_sem, go_sem,
    z_s, z_r, sib_s, sib_r, opp_s, opp_r, near_s, near_r, mid_s, mid_r, ag_s, ag_r, hid_s, hid_r, dg_s, dg_r, fin_s, fin_r,
):
    n_sec, n_row, n_col = sizes
    n_z = n_col // 2
    chunks = n_z
    tok = x_hbm.shape[1]
    span = 2 * tok
    quarter = span // n_row
    feat, width = wg.shape
    sec, row, col = lax.axis_index("section"), lax.axis_index("row"), lax.axis_index("col")
    core, z = col % 2, col // 2
    sibling = {"col": col + 1 - 2 * core}
    before = (sec + n_sec - 1) % n_sec
    after = (sec + 1) % n_sec

    def rows(start, size):
        return pl.ds(pl.multiple_of(start, size), size)

    def turn(k):
        return 1 - 2 * (k % 2)

    def at_row(shift):
        return (row + shift + n_row) % n_row

    def at_z(shift):
        return 2 * ((z + shift + n_z) % n_z) + core

    def offset(k):
        return -((k + 1) // 2) * turn(k)

    def remote(src, dst, send, recv, device):
        return pltpu.make_async_remote_copy(
            src_ref=src, dst_ref=dst, send_sem=send, recv_sem=recv, device_id=device, device_id_type=MESH
        )

    own = rows(tok * core, tok)
    loads = [
        pltpu.make_async_copy(x_hbm.at[0], xg.at[0, own], load_sem.at[0]),
        pltpu.make_async_copy(g_hbm.at[0], xg.at[1, own], load_sem.at[1]),
        pltpu.make_async_copy(wg_hbm.at[0], wg, load_sem.at[2]),
        pltpu.make_async_copy(wu_hbm.at[0], wu, load_sem.at[3]),
        pltpu.make_async_copy(wd_hbm.at[0], wd, load_sem.at[4]),
    ]
    for load in loads:
        load.start()

    barrier = pltpu.get_barrier_semaphore()

    def greet(device):
        pl.semaphore_signal(barrier, inc=1, device_id=device, device_id_type=MESH)

    greet(sibling)
    greet({"row": at_row(1)})
    greet({"row": at_row(-1)})

    greet({"section": before})
    greet({"section": after})

    greet({"col": at_z(1)})
    greet({"col": at_z(-1)})

    acc_g[...] = jnp.zeros_like(acc_g)
    acc_u[...] = jnp.zeros_like(acc_u)
    acc_d[...] = jnp.zeros_like(acc_d)
    loads[0].wait()
    loads[1].wait()
    pl.semaphore_wait(barrier, 7)

    def to_sibling(k, half):
        place = rows(span * k + tok * half, tok)
        return remote(xg.at[:, place], xg.at[:, place], sib_s.at[k], sib_r.at[k], sibling)

    def along_z(k):
        held = rows(span * jnp.maximum(k - 2, 0) + tok * core, tok)
        place = rows(span * k + tok * core, tok)
        return remote(xg.at[:, held], xg.at[:, place], z_s.at[k], z_r.at[k], {"col": at_z(turn(k))})

    def pass_on(k):
        along_z(k).wait_recv()

        @pl.when(k + 2 < chunks)
        def _():
            along_z(k + 2).start()

        to_sibling(k, core).start()

    def opp_copy(k):
        place = rows(quarter * k, quarter)
        return remote(opp_out.at[place], opp_in.at[place], opp_s.at[k], opp_r.at[k], {"row": at_row(turn(k))})

    def near_copy(k):
        place = rows(quarter * k, quarter)
        return remote(near_out.at[place], near_in.at[place], near_s.at[k], near_r.at[k], {"row": at_row(-turn(k))})

    def mid_copy(k):
        place = rows(quarter * k, quarter)
        return remote(mid_out.at[place], mid_in.at[place], mid_s.at[k], mid_r.at[k], {"row": at_row(turn(k))})

    def piece(k, owner):
        return rows(span * k + quarter * owner, quarter)

    def ag_copy(k, slot, owner, target):
        place = piece(k, owner)
        return remote(h.at[place], h.at[place], ag_s.at[3 * k + slot], ag_r.at[3 * k + slot], {"row": target})

    def hid_copy(k, slot, owner, target):
        place = piece(k, owner)
        return remote(hid.at[place], hid.at[place], hid_s.at[3 * k + slot], hid_r.at[3 * k + slot], {"row": target})

    def dg_copy(k):
        return remote(dg_out.at[k], dg_in.at[k], dg_s.at[k], dg_r.at[k], sibling)

    def fin_copy(k):
        target = {"section": before, "col": at_z(offset(k))}
        return remote(fin_out.at[k], fin_in.at[k], fin_s.at[k], fin_r.at[k], target)

    def forward(k):
        to_sibling(k, 1 - core).wait_recv()
        place = rows(span * k, span)
        x, g = xg[0, place, :], xg[1, place, :]

        @pl.when(k == 0)
        def _():
            loads[2].wait()

        part[place, :width] = jnp.dot(x, wg[...], preferred_element_type=F32)

        @pl.when(k == 0)
        def _():
            loads[3].wait()

        part[place, width : 2 * width] = jnp.dot(x, wu[...], preferred_element_type=F32)

        @pl.when(k == 0)
        def _():
            loads[4].wait()

        part[place, 2 * width :] = contract_cols(g, wd[...])
        slot = rows(quarter * k, quarter)
        opp_out[slot] = part[piece(k, at_row(2)), :].astype(BF16)
        opp_copy(k).start()
        near_out[slot] = part[piece(k, at_row(-turn(k))), :].astype(BF16)
        near_copy(k).start()

    def middle(k):
        slot = rows(quarter * k, quarter)
        opp_copy(k).wait_recv()
        mid_out[slot] = (part[piece(k, at_row(turn(k))), :] + opp_in[slot].astype(F32)).astype(BF16)
        mid_copy(k).start()

    def sums(k):
        slot = rows(quarter * k, quarter)
        near_copy(k).wait_recv()
        mid_copy(k).wait_recv()
        mine = piece(k, row)
        total = part[mine, :] + near_in[slot].astype(F32) + mid_in[slot].astype(F32)
        gate, up, grad_hidden = total[:, :width], total[:, width : 2 * width], total[:, 2 * width :]
        sig = jax.nn.sigmoid(gate)
        h[mine, :width] = (grad_hidden * up * sig * (1.0 + gate * (1.0 - sig))).astype(BF16)
        h[mine, width : 2 * width] = (grad_hidden * gate * sig).astype(BF16)
        hid[mine, :] = (gate * sig * up).astype(BF16)
        ag_copy(k, 0, row, at_row(-turn(k))).start()
        ag_copy(k, 1, row, at_row(turn(k))).start()

    def onward(k):
        ag_copy(k, 0, at_row(turn(k)), row).wait_recv()
        ag_copy(k, 2, at_row(turn(k)), at_row(-turn(k))).start()

    def hidden_out(k):
        hid_copy(k, 0, row, at_row(-turn(k))).start()
        hid_copy(k, 1, row, at_row(turn(k))).start()

    def hidden_onward(k):
        hid_copy(k, 0, at_row(turn(k)), row).wait_recv()
        hid_copy(k, 2, at_row(turn(k)), at_row(-turn(k))).start()
        opp_copy(k).wait_send()
        near_copy(k).wait_send()
        mid_copy(k).wait_send()
        ag_copy(k, 0, row, at_row(-turn(k))).wait_send()
        ag_copy(k, 1, row, at_row(turn(k))).wait_send()

    def hidden_in(k):
        hid_copy(k, 1, at_row(-turn(k)), row).wait_recv()
        hid_copy(k, 2, at_row(2), row).wait_recv()
        ag_copy(k, 2, at_row(turn(k)), at_row(-turn(k))).wait_send()
        hid_copy(k, 0, row, at_row(-turn(k))).wait_send()
        hid_copy(k, 1, row, at_row(turn(k))).wait_send()
        hid_copy(k, 2, at_row(turn(k)), at_row(-turn(k))).wait_send()

    def pair(k):
        return rows(span * (k - 1), 2 * span)

    def input_grad(k):
        for q in (k - 1, k):
            ag_copy(q, 1, at_row(-turn(q)), row).wait_recv()
            ag_copy(q, 2, at_row(2), row).wait_recv()
        place = pair(k)
        part[place, :feat] = contract_cols(h[place, :width], wg[...]) + contract_cols(h[place, width:], wu[...])
        for q in (k - 1, k):
            dg_out[q] = part[rows(span * q + tok * (1 - core), tok), :feat]
            dg_copy(q).start()

    def send_grad(k):
        @pl.when(k == 1)
        def _():
            pl.semaphore_wait(go_sem, 1)

        for q in (k - 1, k):
            dg_copy(q).wait_recv()
            fin_out[q] = (part[rows(span * q + tok * core, tok), :feat] + dg_in[q]).astype(BF16)
            fin_copy(q).start()
        for q in (k - 1, k):
            dg_copy(q).wait_send()
            to_sibling(q, core).wait_send()

            @pl.when(q > 0)
            def _():
                along_z(q).wait_send()

    def accumulate(k):
        place = pair(k)
        acc_g[...] += contract_rows(xg[0, place, :], h[place, :width])
        acc_u[...] += contract_rows(xg[0, place, :], h[place, width:])

    def finish(k):
        place = pair(k)
        st_g[0] = (acc_g[...] + contract_rows(xg[0, place, :], h[place, :width])).astype(BF16)
        st_u[0] = (acc_u[...] + contract_rows(xg[0, place, :], h[place, width:])).astype(BF16)

    def accumulate_down(k):
        place = pair(k)
        acc_d[...] += contract_rows(hid[place, :], xg[1, place, :])

    def stage(i, lag, run, extra=None):
        k = i - lag
        ok = (k >= 0) & (k < chunks)
        if extra is not None:
            ok = ok & extra(k)

        @pl.when(ok)
        def _():
            run(k)

    along_z(1).start()
    along_z(2).start()
    to_sibling(0, core).start()

    last = chunks - 1

    def odd(k):
        return k % 2 == 1

    def odd_not_last(k):
        return (k % 2 == 1) & (k < last)

    def step(i, _):
        stage(i, LAG_MID, middle)
        stage(i, LAG_OUT, send_grad, odd)
        stage(i, 0, forward)
        stage(i, LAG_HID_FWD, hidden_onward)
        stage(i, LAG_HID, hidden_out)
        stage(i, LAG_DOWN, hidden_in)
        stage(i, LAG_DOWN, accumulate_down, odd_not_last)
        stage(i, LAG_GRAD, input_grad, odd)
        stage(i, LAG_SUM, sums)
        stage(i, LAG_ACC, accumulate, odd_not_last)
        stage(i, LAG_ACC, finish, lambda k: k == last)
        stage(i, -1, pass_on, lambda k: k > 0)

        @pl.when(i == chunks - 2)
        def _():
            pl.semaphore_signal(go_sem, inc=1, device_id={"section": after}, device_id_type=MESH)

        stage(i, LAG_FWD, onward)
        return 0

    lax.fori_loop(0, chunks + LAG_DOWN, step, 0)

    place = pair(last)
    st_d[0] = (acc_d[...] + contract_rows(hid[place, :], xg[1, place, :])).astype(BF16)
    for k in range(chunks):
        fin_copy(k).wait_recv()
        fin_copy(k).wait_send()
    total = fin_in[0].astype(F32)
    for k in range(1, chunks):
        total = total + fin_in[k].astype(F32)
    or_ref[0] = total.astype(BF16)


def write_out(d_in, g_in, u_in, r_in, d_out, g_out, u_out, r_out, sem):
    pairs = [(d_in, d_out), (g_in, g_out), (u_in, u_out), (r_in, r_out)]
    copies = [pltpu.make_async_copy(src, dst, sem.at[j]) for j, (src, dst) in enumerate(pairs)]
    for copy in copies:
        copy.start()
    for copy in copies:
        copy.wait()


def shards(sizes, layer_input, output_grad, gate_weight, up_weight, down_weight):
    tok, feat = layer_input.shape[1:]
    width = gate_weight.shape[2]
    chunks = sizes[2] // 2
    span = 2 * tok
    total = span * chunks
    quarter_rows = total // sizes[1]
    dma = pltpu.SemaphoreType.DMA
    shapes = [(1, width, feat), (1, feat, width), (1, feat, width), (1, tok, feat)]
    results = pl.pallas_call(
        functools.partial(kernel, sizes),
        out_shape=[pltpu.VMEM(shape, BF16) for shape in shapes],
        in_specs=[pl.BlockSpec(memory_space=pltpu.HBM)] * 5,
        out_specs=[pl.BlockSpec(memory_space=pltpu.VMEM)] * 4,
        scratch_shapes=[
            pltpu.VMEM((feat, width), BF16),
            pltpu.VMEM((feat, width), BF16),
            pltpu.VMEM((width, feat), BF16),
            pltpu.VMEM((2, total, feat), BF16),
            pltpu.VMEM((total, 3 * width), F32),
        ]
        + [pltpu.VMEM((quarter_rows, 3 * width), BF16)] * 6
        + [
            pltpu.VMEM((total, 2 * width), BF16),
            pltpu.VMEM((total, width), BF16),
            pltpu.VMEM((feat, width), F32),
            pltpu.VMEM((feat, width), F32),
            pltpu.VMEM((width, feat), F32),
            pltpu.VMEM((chunks, tok, feat), F32),
            pltpu.VMEM((chunks, tok, feat), F32),
            pltpu.VMEM((chunks, tok, feat), BF16),
            pltpu.VMEM((chunks, tok, feat), BF16),
            dma((5,)),
            pltpu.SemaphoreType.REGULAR,
        ]
        + [dma((chunks,))] * 10
        + [dma((3 * chunks,))] * 4
        + [dma((chunks,))] * 4,
        compiler_params=pltpu.CompilerParams(
            collective_id=0, has_side_effects=True, vmem_limit_bytes=57 * 1024 * 1024
        ),
    )(layer_input, output_grad, gate_weight, up_weight, down_weight)
    return pl.pallas_call(
        write_out,
        out_shape=[jax.ShapeDtypeStruct(shape, BF16) for shape in shapes],
        in_specs=[pl.BlockSpec(memory_space=pl.ANY)] * 4,
        out_specs=[pl.BlockSpec(memory_space=pltpu.HBM)] * 4,
        scratch_shapes=[dma((4,))],
        compiler_params=pltpu.CompilerParams(vmem_limit_bytes=1024 * 1024),
    )(*results)


def solution(mesh):
    sizes = tuple(mesh.shape[axis] for axis in ("section", "row", "col"))
    return jax.shard_map(
        functools.partial(shards, sizes),
        mesh=mesh,
        in_specs=(
            P("section", "col", "row"),
            P("section", "col", "row"),
            P("section", "row", "col"),
            P("section", "row", "col"),
            P("section", "col", "row"),
        ),
        out_specs=(
            P("section", "col", "row"),
            P("section", "row", "col"),
            P("section", "row", "col"),
            P("section", "col", "row"),
        ),
        check_vma=False,
    )
```

```python
import functools

import jax
import jax.numpy as jnp
from jax import lax
from jax.experimental import pallas as pl
from jax.experimental.pallas import tpu as pltpu
from jax.sharding import PartitionSpec as P

MESH = pl.DeviceIdType.MESH
F32 = jnp.float32
BF16 = jnp.bfloat16

LAG_MID, LAG_SUM, LAG_FWD, LAG_GRAD, LAG_ACC, LAG_OUT = 2, 6, 8, 11, 11, 12
LAG_HID, LAG_HID_FWD, LAG_DOWN = 13, 16, 23

FIRST = 2


def contract_cols(left, right):
    return lax.dot_general(left, right, (((1,), (1,)), ((), ())), preferred_element_type=F32)


def contract_rows(left, right):
    return lax.dot_general(left, right, (((0,), (0,)), ((), ())), preferred_element_type=F32)


def kernel(
    sizes,
    x_hbm, g_hbm, wg_hbm, wu_hbm, wd_hbm,
    st_d, st_g, st_u, or_ref,
    wg, wu, wd, xg, part, opp_out, near_out, opp_in, near_in, mid_out, mid_in, h, hid,
    acc_g, acc_u, acc_d, dg_out, dg_in, fin_out, fin_in,
    load_sem, go_sem,
    z_s, z_r, sib_s, sib_r, opp_s, opp_r, near_s, near_r, mid_s, mid_r, ag_s, ag_r, hid_s, hid_r, dg_s, dg_r, fin_s, fin_r,
):
    n_sec, n_row, n_col = sizes
    n_z = n_col // 2
    chunks = n_z
    tok = x_hbm.shape[1]
    span = 2 * tok
    quarter = span // n_row
    feat, width = wg.shape
    sec, row, col = lax.axis_index("section"), lax.axis_index("row"), lax.axis_index("col")
    core, z = col % 2, col // 2
    sibling = {"col": col + 1 - 2 * core}
    before = (sec + n_sec - 1) % n_sec
    after = (sec + 1) % n_sec

    def rows(start, size):
        return pl.ds(pl.multiple_of(start, size), size)

    def turn(k):
        return 1 - 2 * (k % 2)

    def at_row(shift):
        return (row + shift + n_row) % n_row

    def at_z(shift):
        return 2 * ((z + shift + n_z) % n_z) + core

    def offset(k):
        return -((k + 1) // 2) * turn(k)

    def remote(src, dst, send, recv, device):
        return pltpu.make_async_remote_copy(
            src_ref=src, dst_ref=dst, send_sem=send, recv_sem=recv, device_id=device, device_id_type=MESH
        )

    own = rows(tok * core, tok)
    loads = [
        pltpu.make_async_copy(x_hbm.at[0], xg.at[0, own], load_sem.at[0]),
        pltpu.make_async_copy(g_hbm.at[0], xg.at[1, own], load_sem.at[1]),
        pltpu.make_async_copy(wg_hbm.at[0], wg, load_sem.at[2]),
        pltpu.make_async_copy(wu_hbm.at[0], wu, load_sem.at[3]),
        pltpu.make_async_copy(wd_hbm.at[0], wd, load_sem.at[4]),
    ]
    for load in loads:
        load.start()

    barrier = pltpu.get_barrier_semaphore()

    def greet(device):
        pl.semaphore_signal(barrier, inc=1, device_id=device, device_id_type=MESH)

    greet(sibling)
    greet({"row": at_row(1)})
    greet({"row": at_row(-1)})

    greet({"section": before})
    greet({"section": after})

    greet({"col": at_z(1)})
    greet({"col": at_z(-1)})

    acc_g[...] = jnp.zeros_like(acc_g)
    acc_u[...] = jnp.zeros_like(acc_u)
    acc_d[...] = jnp.zeros_like(acc_d)
    loads[0].wait()
    loads[1].wait()
    pl.semaphore_wait(barrier, 7)

    def to_sibling(k, half):
        place = rows(span * k + tok * half, tok)
        return remote(xg.at[:, place], xg.at[:, place], sib_s.at[k], sib_r.at[k], sibling)

    def along_z(k):
        held = rows(span * jnp.maximum(k - 2, 0) + tok * core, tok)
        place = rows(span * k + tok * core, tok)
        return remote(xg.at[:, held], xg.at[:, place], z_s.at[k], z_r.at[k], {"col": at_z(turn(k))})

    def pass_on(k):
        along_z(k).wait_recv()

        @pl.when(k + 2 < chunks)
        def _():
            along_z(k + 2).start()

        to_sibling(k, core).start()

    def opp_copy(k):
        place = rows(quarter * k, quarter)
        return remote(opp_out.at[place], opp_in.at[place], opp_s.at[k], opp_r.at[k], {"row": at_row(turn(k))})

    def near_copy(k):
        place = rows(quarter * k, quarter)
        return remote(near_out.at[place], near_in.at[place], near_s.at[k], near_r.at[k], {"row": at_row(-turn(k))})

    def mid_copy(k):
        place = rows(quarter * k, quarter)
        return remote(mid_out.at[place], mid_in.at[place], mid_s.at[k], mid_r.at[k], {"row": at_row(turn(k))})

    def piece(k, owner):
        return rows(span * k + quarter * owner, quarter)

    def ag_copy(k, slot, owner, target):
        place = piece(k, owner)
        return remote(h.at[place], h.at[place], ag_s.at[3 * k + slot], ag_r.at[3 * k + slot], {"row": target})

    def hid_copy(k, slot, owner, target):
        place = piece(k, owner)
        return remote(hid.at[place], hid.at[place], hid_s.at[3 * k + slot], hid_r.at[3 * k + slot], {"row": target})

    def dg_copy(k):
        return remote(dg_out.at[k], dg_in.at[k], dg_s.at[k], dg_r.at[k], sibling)

    def fin_copy(k):
        target = {"section": before, "col": at_z(offset(k))}
        return remote(fin_out.at[k], fin_in.at[k], fin_s.at[k], fin_r.at[k], target)

    def forward(k):
        to_sibling(k, 1 - core).wait_recv()
        place = rows(span * k, span)
        x, g = xg[0, place, :], xg[1, place, :]

        @pl.when(k == 0)
        def _():
            loads[2].wait()

        part[place, :width] = jnp.dot(x, wg[...], preferred_element_type=F32)

        @pl.when(k == 0)
        def _():
            loads[3].wait()

        part[place, width : 2 * width] = jnp.dot(x, wu[...], preferred_element_type=F32)

        @pl.when(k == 0)
        def _():
            loads[4].wait()

        part[place, 2 * width :] = contract_cols(g, wd[...])
        slot = rows(quarter * k, quarter)
        opp_out[slot] = part[piece(k, at_row(2)), :].astype(BF16)
        opp_copy(k).start()
        near_out[slot] = part[piece(k, at_row(-turn(k))), :].astype(BF16)
        near_copy(k).start()

    def middle(k):
        slot = rows(quarter * k, quarter)
        opp_copy(k).wait_recv()
        mid_out[slot] = (part[piece(k, at_row(turn(k))), :] + opp_in[slot].astype(F32)).astype(BF16)
        mid_copy(k).start()

    def sums(k):
        slot = rows(quarter * k, quarter)
        near_copy(k).wait_recv()
        mid_copy(k).wait_recv()
        mine = piece(k, row)
        total = part[mine, :] + near_in[slot].astype(F32) + mid_in[slot].astype(F32)
        gate, up, grad_hidden = total[:, :width], total[:, width : 2 * width], total[:, 2 * width :]
        sig = jax.nn.sigmoid(gate)
        h[mine, :width] = (grad_hidden * up * sig * (1.0 + gate * (1.0 - sig))).astype(BF16)
        h[mine, width : 2 * width] = (grad_hidden * gate * sig).astype(BF16)
        hid[mine, :] = (gate * sig * up).astype(BF16)
        ag_copy(k, 0, row, at_row(-turn(k))).start()
        ag_copy(k, 1, row, at_row(turn(k))).start()

    def onward(k):
        ag_copy(k, 0, at_row(turn(k)), row).wait_recv()
        ag_copy(k, 2, at_row(turn(k)), at_row(-turn(k))).start()

    def hidden_out(k):
        hid_copy(k, 0, row, at_row(-turn(k))).start()
        hid_copy(k, 1, row, at_row(turn(k))).start()

    def hidden_onward(k):
        hid_copy(k, 0, at_row(turn(k)), row).wait_recv()
        hid_copy(k, 2, at_row(turn(k)), at_row(-turn(k))).start()
        opp_copy(k).wait_send()
        near_copy(k).wait_send()
        mid_copy(k).wait_send()
        ag_copy(k, 0, row, at_row(-turn(k))).wait_send()
        ag_copy(k, 1, row, at_row(turn(k))).wait_send()

    def hidden_in(k):
        hid_copy(k, 1, at_row(-turn(k)), row).wait_recv()
        hid_copy(k, 2, at_row(2), row).wait_recv()
        ag_copy(k, 2, at_row(turn(k)), at_row(-turn(k))).wait_send()
        hid_copy(k, 0, row, at_row(-turn(k))).wait_send()
        hid_copy(k, 1, row, at_row(turn(k))).wait_send()
        hid_copy(k, 2, at_row(turn(k)), at_row(-turn(k))).wait_send()

    def pair(k):
        return rows(span * (k - 1), 2 * span)

    def input_grad(k):
        for q in (k - 1, k):
            ag_copy(q, 1, at_row(-turn(q)), row).wait_recv()
            ag_copy(q, 2, at_row(2), row).wait_recv()
        place = pair(k)
        part[place, :feat] = contract_cols(h[place, :width], wg[...]) + contract_cols(h[place, width:], wu[...])
        for q in (k - 1, k):
            dg_out[q] = part[rows(span * q + tok * (1 - core), tok), :feat]
            dg_copy(q).start()

    def send_grad(k):
        for q in (k - 1, k):
            dg_copy(q).wait_recv()
            fin_out[q] = (part[rows(span * q + tok * core, tok), :feat] + dg_in[q]).astype(BF16)
            fin_copy(q).start()
        for q in (k - 1, k):
            dg_copy(q).wait_send()
            to_sibling(q, core).wait_send()

            @pl.when(q > 0)
            def _():
                along_z(q).wait_send()

    def accumulate(k):
        place = pair(k)
        acc_g[...] += contract_rows(xg[0, place, :], h[place, :width])
        acc_u[...] += contract_rows(xg[0, place, :], h[place, width:])

    def finish(k):
        place = pair(k)
        st_g[0] = (acc_g[...] + contract_rows(xg[0, place, :], h[place, :width])).astype(BF16)
        st_u[0] = (acc_u[...] + contract_rows(xg[0, place, :], h[place, width:])).astype(BF16)

    def accumulate_down(k):
        place = pair(k)
        acc_d[...] += contract_rows(hid[place, :], xg[1, place, :])

    def in_turn(k):
        return (k + FIRST) % chunks

    def stage(i, lag, run, extra=None, turned=False):
        k = i - lag
        ok = (k >= 0) & (k < chunks)
        if extra is not None:
            ok = ok & extra(k)

        @pl.when(ok)
        def _():
            run(in_turn(k) if turned else k)

    along_z(1).start()
    along_z(2).start()
    to_sibling(0, core).start()

    last = chunks - 1

    def may_send(k):
        pl.semaphore_wait(go_sem, 1)

    def odd(k):
        return k % 2 == 1

    def odd_not_last(k):
        return (k % 2 == 1) & (k < last)

    def step(i, _):
        stage(i, LAG_MID, middle)
        stage(i, LAG_OUT, may_send, lambda k: k == 1)
        stage(i, LAG_OUT, send_grad, odd, True)
        stage(i, 0, forward)
        stage(i, LAG_HID_FWD, hidden_onward, None, True)
        stage(i, LAG_HID, hidden_out, None, True)
        stage(i, LAG_DOWN, hidden_in, None, True)
        stage(i, LAG_DOWN, accumulate_down, odd_not_last, True)
        stage(i, LAG_GRAD, input_grad, odd, True)
        stage(i, LAG_SUM, sums, None, True)
        stage(i, LAG_ACC, accumulate, odd_not_last, True)
        stage(i, LAG_ACC, finish, lambda k: k == last, True)
        stage(i, -1, pass_on, lambda k: k > 0)

        @pl.when(i == chunks - 2)
        def _():
            pl.semaphore_signal(go_sem, inc=1, device_id={"section": after}, device_id_type=MESH)

        stage(i, LAG_FWD, onward, None, True)
        return 0

    lax.fori_loop(0, chunks + LAG_DOWN, step, 0)

    place = pair(in_turn(last))
    st_d[0] = (acc_d[...] + contract_rows(hid[place, :], xg[1, place, :])).astype(BF16)
    for k in range(chunks):
        fin_copy(k).wait_recv()
        fin_copy(k).wait_send()
    total = fin_in[0].astype(F32)
    for k in range(1, chunks):
        total = total + fin_in[k].astype(F32)
    or_ref[0] = total.astype(BF16)


def write_out(d_in, g_in, u_in, r_in, d_out, g_out, u_out, r_out, sem):
    pairs = [(d_in, d_out), (g_in, g_out), (u_in, u_out), (r_in, r_out)]
    copies = [pltpu.make_async_copy(src, dst, sem.at[j]) for j, (src, dst) in enumerate(pairs)]
    for copy in copies:
        copy.start()
    for copy in copies:
        copy.wait()


def shards(sizes, layer_input, output_grad, gate_weight, up_weight, down_weight):
    tok, feat = layer_input.shape[1:]
    width = gate_weight.shape[2]
    chunks = sizes[2] // 2
    span = 2 * tok
    total = span * chunks
    quarter_rows = total // sizes[1]
    dma = pltpu.SemaphoreType.DMA
    shapes = [(1, width, feat), (1, feat, width), (1, feat, width), (1, tok, feat)]
    results = pl.pallas_call(
        functools.partial(kernel, sizes),
        out_shape=[pltpu.VMEM(shape, BF16) for shape in shapes],
        in_specs=[pl.BlockSpec(memory_space=pltpu.HBM)] * 5,
        out_specs=[pl.BlockSpec(memory_space=pltpu.VMEM)] * 4,
        scratch_shapes=[
            pltpu.VMEM((feat, width), BF16),
            pltpu.VMEM((feat, width), BF16),
            pltpu.VMEM((width, feat), BF16),
            pltpu.VMEM((2, total, feat), BF16),
            pltpu.VMEM((total, 3 * width), F32),
        ]
        + [pltpu.VMEM((quarter_rows, 3 * width), BF16)] * 6
        + [
            pltpu.VMEM((total, 2 * width), BF16),
            pltpu.VMEM((total, width), BF16),
            pltpu.VMEM((feat, width), F32),
            pltpu.VMEM((feat, width), F32),
            pltpu.VMEM((width, feat), F32),
            pltpu.VMEM((chunks, tok, feat), F32),
            pltpu.VMEM((chunks, tok, feat), F32),
            pltpu.VMEM((chunks, tok, feat), BF16),
            pltpu.VMEM((chunks, tok, feat), BF16),
            dma((5,)),
            pltpu.SemaphoreType.REGULAR,
        ]
        + [dma((chunks,))] * 10
        + [dma((3 * chunks,))] * 4
        + [dma((chunks,))] * 4,
        compiler_params=pltpu.CompilerParams(
            collective_id=0, has_side_effects=True, vmem_limit_bytes=57 * 1024 * 1024
        ),
    )(layer_input, output_grad, gate_weight, up_weight, down_weight)
    return pl.pallas_call(
        write_out,
        out_shape=[jax.ShapeDtypeStruct(shape, BF16) for shape in shapes],
        in_specs=[pl.BlockSpec(memory_space=pl.ANY)] * 4,
        out_specs=[pl.BlockSpec(memory_space=pltpu.HBM)] * 4,
        scratch_shapes=[dma((4,))],
        compiler_params=pltpu.CompilerParams(vmem_limit_bytes=1024 * 1024),
    )(*results)


def solution(mesh):
    sizes = tuple(mesh.shape[axis] for axis in ("section", "row", "col"))
    return jax.shard_map(
        functools.partial(shards, sizes),
        mesh=mesh,
        in_specs=(
            P("section", "col", "row"),
            P("section", "col", "row"),
            P("section", "row", "col"),
            P("section", "row", "col"),
            P("section", "col", "row"),
        ),
        out_specs=(
            P("section", "col", "row"),
            P("section", "row", "col"),
            P("section", "row", "col"),
            P("section", "col", "row"),
        ),
        check_vma=False,
    )
```
